128 devices in a mesh: fsdp: 8 (over y_lo, z), replica: 16 (over y_hi, x, core).
Axes of the slice: x: 4, y: 4 (y_hi: 2, y_lo: 2; y = y_hi * 2 + y_lo), z: 4, core: 2. Of those that a mesh axis runs over, the one named last changes fastest.
Arguments:
- out_weight: bfloat16 [2, 512, 16384], P(None, None, 'fsdp'), may hold values from -6 to 6
- down_weight: bfloat16 [2, 1024, 16384], P(None, None, 'fsdp'), may hold values from -6 to 6
- layer_share: int32 [16], replicated, may hold values from 0 to 15, each once
- rank_map: int32 [8], replicated, may hold values from 0 to 7, each once
Outputs:
- out_quant: bfloat16 [8, 128, 16384], P('fsdp')
- out_scales: bfloat16 [8, 128, 128], P('fsdp')
- down_quant: bfloat16 [8, 256, 16384], P('fsdp')
- down_scales: bfloat16 [8, 256, 128], P('fsdp')
The draws below stay inside these ranges and needn't reach their ends.
Inputs may be any that keep to these rules, and one draw needn't show every extreme that they name: `layer_share`: each block number appears once. `rank_map`: each rank appears once.
All inputs are finite; a program needn't handle non-finite values.
Results may differ from the reference program's by a relative error of at most 0.012.
Values may be sent and summed in bfloat16 or wider, within the bound.
No kernel may reach another device: no remote copies, remote signals or barrier semaphores. Data moves between devices by JAX's collectives and lax.ppermute only.
A program may use at most 128 MiB of HBM per device.

```python
import math
import jax
import jax.numpy as jnp
from jax import lax

D = 16384
LAYERS = 2
ROWS_O = 512
ROWS_DOWN = 1024
N_FSDP = 8
N_REPLICA = 16


def block_levels(stream_key, extent, pieces, smallest, high):
    def one(position, shards_of):
        steps = jax.random.uniform(jax.random.fold_in(jax.random.fold_in(stream_key, 6), position), (shards_of,), jnp.float32, smallest / len(pieces), high / len(pieces))
        return jnp.repeat(jnp.exp(steps), extent[position] // shards_of).reshape((-1,) + (1,) * (len(extent) - position - 1))

    level = one(*pieces[0])
    for cut in pieces[1:]:
        level = level * one(*cut)
    return level


def centred(stream_key, shape, deviation, most, pieces=(), kind=jnp.bfloat16):
    loudness = block_levels(stream_key, shape, pieces, -0.22, 0.18) if pieces else 1.0
    result = jax.random.normal(stream_key, shape, jnp.float32) * deviation * loudness
    return jnp.minimum(jnp.maximum(result, -most), most).astype(kind)


def setup_inputs(seed: int = 0) -> dict:
    key_of = jax.random.split(jax.random.key(seed), 5)
    return {
        "out_weight": centred(key_of[0], (LAYERS, ROWS_O, D), 1.0, 6.0, ((2, 8),)),
        "down_weight": centred(key_of[1], (LAYERS, ROWS_DOWN, D), 1.0, 6.0, ((2, 8),)),
        "layer_share": jax.random.permutation(key_of[2], N_REPLICA).astype(jnp.int32),
        "rank_map": jax.random.permutation(key_of[3], N_FSDP).astype(jnp.int32),
    }


def sylvester(order):
    index = jnp.arange(order, dtype=jnp.int32)
    signs = jnp.ones((order, order), jnp.float32)
    level = 1
    while level < order:
        bit_row = index // level % 2
        signs = signs * (1 - 2 * (bit_row[:, None] * bit_row[None, :])).astype(jnp.float32)
        level = level * 2
    return signs / math.sqrt(order)

def rotate_cast(weights_in):
    columns = weights_in.shape[-1]
    side_len = math.isqrt(columns)
    rotation = sylvester(side_len)
    squares = weights_in.reshape(-1, side_len, side_len).astype(jnp.float32)
    half_turn = jnp.einsum('ab,nbc->nac', rotation, squares, precision=lax.Precision.HIGHEST)
    rotated = jnp.einsum('nac,cd->nad', half_turn, rotation, precision=lax.Precision.HIGHEST)
    largest = lax.optimization_barrier(jnp.max(jnp.abs(rotated), axis=2, keepdims=True))
    block_scale = (largest + 1e-06).astype(jnp.bfloat16)
    quantized = (rotated / block_scale.astype(jnp.float32)).astype(jnp.bfloat16)
    return (quantized.reshape(weights_in.shape), block_scale.reshape(weights_in.shape[:-1] + (side_len,)))

def arrange(weights, layer_share, rank_map):
    layers_all, rows_all, columns = weights.shape
    rank_rows = rows_all // N_FSDP
    stream = weights.reshape(layers_all, N_FSDP, rank_rows, columns).transpose(1, 0, 2, 3)
    stream = stream.reshape(N_FSDP, N_REPLICA, layers_all * rank_rows // N_REPLICA, columns)
    stream = jnp.take(stream, layer_share, axis=1)
    stream = jnp.take(stream, rank_map, axis=0)
    return stream.reshape(N_FSDP, layers_all * rank_rows, columns)

def reference(out_weight, down_weight, layer_share, rank_map):
    out_quant, out_scales = rotate_cast(arrange(out_weight, layer_share, rank_map))
    down_quant, down_scales = rotate_cast(arrange(down_weight, layer_share, rank_map))
    return (out_quant, out_scales, down_quant, down_scales)
```

```python
import functools
import math

import jax
import jax.numpy as jnp
import numpy as np
from jax import lax
from jax.experimental import pallas as pl
from jax.experimental.pallas import tpu as pltpu
from jax.sharding import PartitionSpec as P

SIDE = 128
UNIT = 16
LOCAL = 2048
BLOCKS = LOCAL // SIDE
SHARDS = 8
PARTS = ((0, 1, 0, 2), (1, 1, 2, 2))
VMEM = 40 * 2**20


def signs(order):
    h = np.ones((1, 1), np.float32)
    while h.shape[0] < order:
        h = np.block([[h, h], [h, -h]])
    return h


def two_blocks():
    h = signs(SIDE)
    z = np.zeros_like(h)
    return jnp.asarray(np.block([[h, z], [z, h]]), jnp.bfloat16)


def butterflies(values):
    span = 1
    values = list(values)
    while span < len(values):
        for i in range(len(values)):
            if i & span == 0:
                lo, hi = values[i], values[i + span]
                values[i], values[i + span] = lo + hi, lo - hi
        span *= 2
    return values


def pick_kernel(part, share, ranks, q_ref, out_hbm, down_hbm, send, pairs, sems):
    o0, no, d0, nd = part
    q = q_ref[0]
    copies = []
    for u in range(no):
        for h in range(2):
            block = share[4 * q + 2 * (o0 + u) + h]
            for f in range(SHARDS):
                row = ranks[f] * 64 + lax.rem(block, 8) // 2 * 16
                c = pltpu.make_async_copy(
                    out_hbm.at[block // 8, pl.ds(pl.multiple_of(row, 16), 16), :],
                    pairs.at[u, h, f],
                    sems.at[len(copies)],
                )
                c.start()
                copies.append(c)
    for u in range(nd):
        block = share[4 * q + d0 + u]
        for f in range(SHARDS):
            row = ranks[f] * 128 + lax.rem(block, 8) * 16
            c = pltpu.make_async_copy(
                down_hbm.at[block // 8, pl.ds(pl.multiple_of(row, 16), 16), :],
                send.at[f, pl.ds((no + u) * UNIT, UNIT), :],
                sems.at[len(copies)],
            )
            c.start()
            copies.append(c)
    for c in copies:
        c.wait()
    for u in range(no):
        odd = [lax.rem(share[4 * q + 2 * (o0 + u) + h], 2) == 1 for h in range(2)]
        for f in range(SHARDS):
            halves = []
            for h in range(2):
                rows = pairs[u, h, f].astype(jnp.float32)
                halves.append(jnp.where(odd[h], rows[8:], rows[:8]))
            send[f, pl.ds(u * UNIT, UNIT), :] = jnp.concatenate(halves, 0).astype(
                jnp.bfloat16
            )


def pick(part, share, ranks, q, out_weight, down_weight):
    o0, no, d0, nd = part
    n = (no * 2 + nd) * SHARDS
    shape = (SHARDS, (no + nd) * UNIT, LOCAL)
    return pl.pallas_call(
        functools.partial(pick_kernel, part),
        grid_spec=pltpu.PrefetchScalarGridSpec(
            num_scalar_prefetch=3,
            grid=(),
            in_specs=[pl.BlockSpec(memory_space=pl.ANY)] * 2,
            out_specs=pl.BlockSpec(memory_space=pltpu.VMEM),
            scratch_shapes=[
                pltpu.VMEM((max(no, 1), 2, SHARDS, UNIT, LOCAL), jnp.bfloat16),
                pltpu.SemaphoreType.DMA((n,)),
            ],
        ),
        out_shape=jax.ShapeDtypeStruct(shape, jnp.bfloat16),
        compiler_params=pltpu.CompilerParams(vmem_limit_bytes=VMEM),
        cost_estimate=pl.CostEstimate(
            flops=0, bytes_accessed=3 * math.prod(shape) * 2, transcendentals=0
        ),
        name="pick_rows",
    )(share, ranks, q, out_weight, down_weight)


def rotate_unit(refs, rot, quant, scales, work):
    first = 0
    for ref in refs:

        def shard(s, _, ref=ref, first=first):
            x = ref[s]
            stack = jnp.concatenate(
                [x[:, c * 256 : (c + 1) * 256] for c in range(BLOCKS // 2)], 0
            )
            y = jnp.dot(stack, rot, preferred_element_type=jnp.float32)
            parts = [
                y[c * UNIT : (c + 1) * UNIT, h * SIDE : (h + 1) * SIDE]
                for c in range(BLOCKS // 2)
                for h in range(2)
            ]
            parts = butterflies(parts)
            for k in range(BLOCKS):
                work[(first + s) * BLOCKS + k] = parts[k]
            return 0

        lax.fori_loop(0, ref.shape[0], shard, 0)
        first += ref.shape[0]

    lane = lax.broadcasted_iota(jnp.int32, (UNIT, SIDE), 1)

    def column(k, top):
        parts = butterflies([work[f * BLOCKS + k] for f in range(SHARDS)])
        for f in range(SHARDS):
            a = f * BLOCKS + k
            y = parts[f]
            m = jnp.max(jnp.abs(y), axis=1, keepdims=True) * (1.0 / SIDE)
            s = (m + 1e-06).astype(jnp.bfloat16).astype(jnp.float32)
            r = 1.0 / (s * SIDE)
            quant[:, pl.ds(pl.multiple_of(a * SIDE, SIDE), SIDE)] = (y * r).astype(
                jnp.bfloat16
            )
            top = jnp.where(lane == a, m, top)
        return top

    top = lax.fori_loop(0, BLOCKS, column, jnp.zeros((UNIT, SIDE), jnp.float32))
    scales[...] = (top + 1e-06).astype(jnp.bfloat16)


def rotate_kernel(counts, no, nd, n_alias, q_ref, *refs):
    groups, at = [], 0
    for n in counts:
        groups.append(refs[at : at + n])
        at += n
    rot_ref = refs[at]
    at += 1 + n_alias
    outs = refs[at : at + 4]
    work = refs[at + 4]
    u, g = pl.program_id(0), pl.program_id(1)
    for i, group in enumerate(groups):

        @pl.when((g == i) & (u < no))
        def _(group=group):
            rotate_unit(group, rot_ref[...], outs[0], outs[1], work)

        @pl.when((g == i) & (u >= no))
        def _(group=group):
            rotate_unit(group, rot_ref[...], outs[2], outs[3], work)


def rotate(part, groups, qs, rot, before):
    o0, no, d0, nd = part
    n_groups = len(groups)
    flat = [b for group in groups for b in group]

    def out_at(u, g, q):
        last = u >= no
        return (
            jnp.where(last, 2 * q[n_groups - 1] + o0 + no - 1, 2 * q[g] + o0 + u),
            0,
        )

    def down_at(u, g, q):
        early = u < no
        return jnp.where(early, 4 * q[0] + d0, 4 * q[g] + d0 + u - no), 0

    in_specs = [
        pl.BlockSpec((b.shape[0], UNIT, LOCAL), lambda u, g, q: (0, u, 0)) for b in flat
    ]
    in_specs.append(pl.BlockSpec((256, 256), lambda u, g, q: (0, 0)))
    operands = flat + [rot]
    aliases = {}
    if before is not None:
        for i, b in enumerate(before):
            aliases[1 + len(operands)] = i
            operands.append(b)
            in_specs.append(pl.BlockSpec(memory_space=pl.ANY))
    columns = SHARDS * LOCAL
    shapes = [(128, columns), (128, SIDE), (256, columns), (256, SIDE)]
    maps = [out_at, out_at, down_at, down_at]
    elements = n_groups * (no + nd) * UNIT * columns
    return pl.pallas_call(
        functools.partial(
            rotate_kernel, [len(g) for g in groups], no, nd, len(aliases)
        ),
        grid_spec=pltpu.PrefetchScalarGridSpec(
            num_scalar_prefetch=1,
            grid=(no + nd, n_groups),
            in_specs=in_specs,
            out_specs=[
                pl.BlockSpec((UNIT, s[1]), m) for s, m in zip(shapes, maps)
            ],
            scratch_shapes=[
                pltpu.VMEM((SHARDS * BLOCKS, UNIT, SIDE), jnp.float32)
            ],
        ),
        out_shape=[jax.ShapeDtypeStruct(s, jnp.bfloat16) for s in shapes],
        input_output_aliases=aliases,
        compiler_params=pltpu.CompilerParams(vmem_limit_bytes=VMEM),
        cost_estimate=pl.CostEstimate(
            flops=elements * 256, bytes_accessed=elements * 4, transcendentals=0
        ),
        name="rotate_cast",
    )(qs, *operands)


def replica_steps(step):
    pairs = []
    for y in range(2):
        for x in range(4):
            for c in range(2):
                y2, x2, c2 = step(y, x, c)
                pairs.append(((y * 4 + x) * 2 + c, (y2 * 4 + x2 % 4) * 2 + c2))
    return pairs


RIGHT = replica_steps(lambda y, x, c: (y, x + 1, c))
LEFT = replica_steps(lambda y, x, c: (y, x + 3, c))
OTHER = replica_steps(lambda y, x, c: (y, x, 1 - c))


def shards(out_weight, down_weight, layer_share, rank_map):
    here = lax.axis_index("replica")
    q = here % 4
    qs = lambda *flips: jnp.stack([q ^ f for f in flips]).astype(jnp.int32)
    rot = two_blocks()
    sends = [
        pick(part, layer_share, rank_map, qs(0), out_weight, down_weight)
        for part in PARTS
    ]
    done = None
    half = SHARDS // 2
    late = []
    for part, send in zip(PARTS, sends):
        own = lax.all_to_all(send, "fsdp", split_axis=0, concat_axis=0, tiled=True)
        from_left = lax.ppermute(own[:half], "replica", RIGHT)
        from_right = lax.ppermute(own[half:], "replica", LEFT)
        other = lax.ppermute(own, "replica", OTHER)
        other_left = lax.ppermute(from_left, "replica", OTHER)
        other_right = lax.ppermute(from_right, "replica", OTHER)
        late.append((part, own, other, from_left, from_right, other_left, other_right))
    for part, own, other, l, r, ol, orr in late:
        done = rotate(part, [[own], [other]], qs(0, 1), rot, done)
        done = rotate(part, [[l, r], [ol, orr]], qs(2, 3), rot, done)
    return tuple(d[None] for d in done)


def solution(mesh):
    return jax.shard_map(
        shards,
        mesh=mesh,
        in_specs=(P(None, None, "fsdp"), P(None, None, "fsdp"), P(), P()),
        out_specs=(P("fsdp", None, None),) * 4,
        check_vma=False,
    )
```

```python
import functools
import math

import jax
import jax.numpy as jnp
import numpy as np
from jax import lax
from jax.experimental import pallas as pl
from jax.experimental.pallas import tpu as pltpu
from jax.sharding import PartitionSpec as P

SIDE = 128
UNIT = 16
LOCAL = 2048
BLOCKS = LOCAL // SIDE
SHARDS = 8
PARTS = ((0, 0, 0, 3), (0, 2, 3, 0), (2, 0, 3, 1))
VMEM = 60 * 2**20


def signs(order):
    h = np.ones((1, 1), np.float32)
    while h.shape[0] < order:
        h = np.block([[h, h], [h, -h]])
    return h


def two_blocks():
    h = signs(SIDE)
    z = np.zeros_like(h)
    return jnp.asarray(np.block([[h, z], [z, h]]) / SIDE, jnp.bfloat16)


def butterflies(values):
    span = 1
    values = list(values)
    while span < len(values):
        for i in range(len(values)):
            if i & span == 0:
                lo, hi = values[i], values[i + span]
                values[i], values[i + span] = lo + hi, lo - hi
        span *= 2
    return values


def pick_kernel(part, share, ranks, q_ref, out_hbm, down_hbm, send, pairs, stage, sems, gone):
    o0, no, d0, nd = part
    q = q_ref[0]
    n = 2 * no + nd
    copies = []
    for f in range(SHARDS):
        mine = []
        for u in range(no):
            for h in range(2):
                block = share[4 * q + 2 * (o0 + u) + h]
                row = ranks[f] * 64 + lax.rem(block, 8) // 2 * 16
                mine.append(
                    pltpu.make_async_copy(
                        out_hbm.at[block // 8, pl.ds(pl.multiple_of(row, 16), 16), :],
                        pairs.at[u, h, f],
                        sems.at[f * n + len(mine)],
                    )
                )
        for u in range(nd):
            block = share[4 * q + d0 + u]
            row = ranks[f] * 128 + lax.rem(block, 8) * 16
            mine.append(
                pltpu.make_async_copy(
                    down_hbm.at[block // 8, pl.ds(pl.multiple_of(row, 16), 16), :],
                    stage.at[f, pl.ds((no + u) * UNIT, UNIT), :],
                    sems.at[f * n + len(mine)],
                )
            )
        for c in mine:
            c.start()
        copies.append(mine)
    odd = [
        [lax.rem(share[4 * q + 2 * (o0 + u) + h], 2) == 1 for h in range(2)]
        for u in range(no)
    ]
    leaving = []
    for f in range(SHARDS):
        for c in copies[f]:
            c.wait()
        for u in range(no):
            halves = []
            for h in range(2):
                rows = pairs[u, h, f].astype(jnp.float32)
                halves.append(jnp.where(odd[u][h], rows[8:], rows[:8]))
            stage[f, pl.ds(u * UNIT, UNIT), :] = jnp.concatenate(halves, 0).astype(
                jnp.bfloat16
            )
        c = pltpu.make_async_copy(stage.at[f], send.at[f], gone.at[f])
        c.start()
        leaving.append(c)
    for c in leaving:
        c.wait()


def pick(part, share, ranks, q, out_weight, down_weight):
    o0, no, d0, nd = part
    n = (no * 2 + nd) * SHARDS
    shape = (SHARDS, (no + nd) * UNIT, LOCAL)
    return pl.pallas_call(
        functools.partial(pick_kernel, part),
        grid_spec=pltpu.PrefetchScalarGridSpec(
            num_scalar_prefetch=3,
            grid=(),
            in_specs=[pl.BlockSpec(memory_space=pltpu.HBM)] * 2,
            out_specs=pl.BlockSpec(memory_space=pltpu.HBM),
            scratch_shapes=[
                pltpu.VMEM((max(no, 1), 2, SHARDS, UNIT, LOCAL), jnp.bfloat16),
                pltpu.VMEM(shape, jnp.bfloat16),
                pltpu.SemaphoreType.DMA((n,)),
                pltpu.SemaphoreType.DMA((SHARDS,)),
            ],
        ),
        out_shape=jax.ShapeDtypeStruct(shape, jnp.bfloat16),
        compiler_params=pltpu.CompilerParams(vmem_limit_bytes=VMEM),
        cost_estimate=pl.CostEstimate(
            flops=0, bytes_accessed=3 * math.prod(shape) * 2, transcendentals=0
        ),
        name="pick_rows",
    )(share, ranks, q, out_weight, down_weight)


def spread(refs, rot, work):
    first = 0
    for ref in refs:
        for s in range(ref.shape[0]):
            x = ref[s]
            stack = jnp.concatenate(
                [x[:, c * 256 : (c + 1) * 256] for c in range(BLOCKS // 2)], 0
            )
            y = jnp.dot(stack, rot, preferred_element_type=jnp.float32)
            parts = butterflies(
                y[c * UNIT : (c + 1) * UNIT, h * SIDE : (h + 1) * SIDE]
                for c in range(BLOCKS // 2)
                for h in range(2)
            )
            for k in range(BLOCKS):
                work[first + k] = parts[k]
            first += BLOCKS


def finish(quant, scales, work):
    lane = lax.broadcasted_iota(jnp.int32, (UNIT, SIDE), 1)
    top = jnp.zeros((UNIT, SIDE), jnp.float32)
    for k in range(BLOCKS):
        parts = butterflies(work[f * BLOCKS + k] for f in range(SHARDS))
        for f in range(SHARDS):
            a = f * BLOCKS + k
            m = jnp.max(jnp.abs(parts[f]), axis=1, keepdims=True)
            s = (m + 1e-06).astype(jnp.bfloat16).astype(jnp.float32)
            quant[:, a * SIDE : (a + 1) * SIDE] = (parts[f] * (1.0 / s)).astype(
                jnp.bfloat16
            )
            top = jnp.where(lane == a, m, top)
    scales[...] = (top + 1e-06).astype(jnp.bfloat16)


def rotate_kernel(counts, no, nd, n_alias, q_ref, *refs):
    groups, at = [], 0
    for n in counts:
        groups.append(refs[at : at + n])
        at += n
    rot_ref = refs[at]
    at += 1 + n_alias
    work = refs[-1]
    outs = list(refs[at:-1])
    u, g = pl.program_id(0), pl.program_id(1)
    for i, group in enumerate(groups):

        @pl.when(g == i)
        def _(group=group):
            spread(group, rot_ref[...], work)

    if no:

        @pl.when(u < no)
        def _(quant=outs.pop(0), scales=outs.pop(0)):
            finish(quant, scales, work)

    if nd:

        @pl.when(u >= no)
        def _(quant=outs.pop(0), scales=outs.pop(0)):
            finish(quant, scales, work)


def rotate(part, groups, q_here, flips, rot, before):
    o0, no, d0, nd = part
    n_groups = len(groups)
    flat = [b for group in groups for b in group]

    def sharer(q, g):
        return q[0] ^ (flips[0] + g)

    def out_at(u, g, q):
        last = u >= no
        g = jnp.where(last, n_groups - 1, g)
        return 2 * sharer(q, g) + o0 + jnp.where(last, no - 1, u), 0

    def down_at(u, g, q):
        early = u < no
        g = jnp.where(early, 0, g)
        return 4 * sharer(q, g) + d0 + jnp.where(early, 0, u - no), 0

    in_specs = [
        pl.BlockSpec((b.shape[0], UNIT, LOCAL), lambda u, g, q: (0, u, 0)) for b in flat
    ]
    in_specs.append(pl.BlockSpec((256, 256), lambda u, g, q: (0, 0)))
    operands = flat + [rot]
    columns = SHARDS * LOCAL
    shapes = [(128, columns), (128, SIDE), (256, columns), (256, SIDE)]
    maps = [out_at, out_at, down_at, down_at]
    used = [i for i in range(4) if (no, no, nd, nd)[i]]
    aliases = {}
    for i, t in enumerate(used):
        if before[t] is not None:
            aliases[1 + len(operands)] = i
            operands.append(before[t])
            in_specs.append(pl.BlockSpec(memory_space=pltpu.HBM))
    elements = n_groups * (no + nd) * UNIT * columns
    results = pl.pallas_call(
        functools.partial(
            rotate_kernel, [len(g) for g in groups], no, nd, len(aliases)
        ),
        grid_spec=pltpu.PrefetchScalarGridSpec(
            num_scalar_prefetch=1,
            grid=(no + nd, n_groups),
            in_specs=in_specs,
            out_specs=[pl.BlockSpec((UNIT, shapes[t][1]), maps[t]) for t in used],
            scratch_shapes=[
                pltpu.VMEM((SHARDS * BLOCKS, UNIT, SIDE), jnp.float32)
            ],
        ),
        out_shape=[jax.ShapeDtypeStruct(shapes[t], jnp.bfloat16) for t in used],
        input_output_aliases=aliases,
        compiler_params=pltpu.CompilerParams(vmem_limit_bytes=VMEM),
        cost_estimate=pl.CostEstimate(
            flops=elements * 256, bytes_accessed=elements * 4, transcendentals=0
        ),
        name="rotate_cast",
    )(q_here, *operands)
    after = list(before)
    for t, r in zip(used, results):
        after[t] = r
    return after


def replica_steps(step):
    pairs = []
    for y in range(2):
        for x in range(4):
            for c in range(2):
                y2, x2, c2 = step(y, x, c)
                pairs.append(((y * 4 + x) * 2 + c, (y2 * 4 + x2 % 4) * 2 + c2))
    return pairs


ALONG = replica_steps(lambda y, x, c: (y, x + 1 + 2 * c, c))
OTHER = replica_steps(lambda y, x, c: (y, x, 1 - c))


def shards(out_weight, down_weight, layer_share, rank_map):
    here = lax.axis_index("replica")
    q = (here % 4).astype(jnp.int32)[None]
    rot = two_blocks()
    sends = [
        pick(part, layer_share, rank_map, q, out_weight, down_weight)
        for part in PARTS
    ]
    def swap(value):
        return lax.ppermute(value, "replica", OTHER)

    def exchange(own):
        return swap(own), lax.ppermute(own, "replica", ALONG)

    def to_owner(send):
        return lax.all_to_all(send, "fsdp", split_axis=0, concat_axis=0, tiled=True)

    def near(k, own, other, done):
        return rotate(PARTS[k], [[own], [other]], q, (0, 1), rot, done)

    def far(k, along, along_other, done):
        return rotate(PARTS[k], [[along], [along_other]], q, (2, 3), rot, done)

    def tied(value, *others):
        return lax.optimization_barrier((value,) + others)

    done = [None] * 4
    own0 = to_owner(sends[0])
    send1, own0 = tied(sends[1], own0)
    other0, along0 = exchange(own0)
    along_other0 = swap(along0)
    own1 = to_owner(send1)
    done = near(0, own0, other0, done)
    send2, own1, done[2] = tied(sends[2], own1, done[2])
    other1, along1 = exchange(own1)
    along_other1 = swap(along1)
    own2 = to_owner(send2)
    done = near(1, own1, other1, done)
    own2, done[0] = tied(own2, done[0])
    other2, along2 = exchange(own2)
    done = far(0, along0, along_other0, done)
    along2, done[2] = tied(along2, done[2])
    along_other2 = swap(along2)
    done = near(2, own2, other2, done)
    done = far(1, along1, along_other1, done)
    done = far(2, along2, along_other2, done)
    return tuple(d[None] for d in done)


def solution(mesh):
    return jax.shard_map(
        shards,
        mesh=mesh,
        in_specs=(P(None, None, "fsdp"), P(None, None, "fsdp"), P(), P()),
        out_specs=(P("fsdp", None, None),) * 4,
        check_vma=False,
    )
```

```python
import functools
import itertools
import math

import jax
import jax.numpy as jnp
import numpy as np
from jax import lax
from jax.experimental import pallas as pl
from jax.experimental.pallas import tpu as pltpu
from jax.sharding import PartitionSpec as P

SIDE = 128
UNIT = 16
LOCAL = 2048
BLOCKS = LOCAL // SIDE
SHARDS = 8
PARTS = ((0, 0, 0, 8), (0, 2, 8, 8), (2, 6, 16, 0))
FLIPPED = (0, 0, 0)
FETCH = (
    ((0, 1, 0), (0, 3, 0)),
    ((1, 3, 0), (1, 1, 1)),
    ((0, 2, 0), (1, 2, 1)),
    ((1, 0, 0), None),
)
VMEM = 60 * 2**20


def signs(order):
    h = np.ones((1, 1), np.float32)
    while h.shape[0] < order:
        h = np.block([[h, h], [h, -h]])
    return h


def two_blocks():
    h = signs(SIDE)
    z = np.zeros_like(h)
    return jnp.asarray(np.block([[h, z], [z, h]]) / SIDE, jnp.bfloat16)


def butterflies(values):
    span = 1
    values = list(values)
    while span < len(values):
        for i in range(len(values)):
            if i & span == 0:
                lo, hi = values[i], values[i + span]
                values[i], values[i + span] = lo + hi, lo - hi
        span *= 2
    return values


def by_role(role, values):
    result = jnp.int32(values[3])
    for r in range(3):
        result = jnp.where(role == r, values[r], result)
    return result


def shard_at(here, role, slot, back):
    steps = [FETCH[r][slot] or (0, 0, 0) for r in range(4)]
    dy = by_role(role, [s[0] for s in steps])
    dz = by_role(role, [(4 - s[1]) % 4 if back else s[1] for s in steps])
    return ((here // 4) ^ dy) * 4 + ((here + dz) & 3)


def pick_kernel(part, share, ranks, f_ref, r_ref, out_hbm, down_hbm, *refs):
    o0, no, d0, nd = part
    n = no + nd
    sends, (pairs, stage, sems, gone) = refs[:3], refs[3:]
    here, role = f_ref[0], r_ref[0]
    to = [shard_at(here, role, slot, True) for slot in range(2)] + [here]
    copies = []
    for i in range(3):
        rank = ranks[to[i]]
        mine = []
        for u in range(no):
            for h in range(2):
                block = share[2 * (o0 + u) + h]
                row = rank * 64 + lax.rem(block, 8) // 2 * 16
                mine.append(
                    pltpu.make_async_copy(
                        out_hbm.at[block // 8, pl.ds(pl.multiple_of(row, 16), 16), :],
                        pairs.at[i, u, h],
                        sems.at[i, len(mine)],
                    )
                )
        for u in range(nd):
            block = share[d0 + u]
            row = rank * 128 + lax.rem(block, 8) * 16
            mine.append(
                pltpu.make_async_copy(
                    down_hbm.at[block // 8, pl.ds(pl.multiple_of(row, 16), 16), :],
                    stage.at[i, u],
                    sems.at[i, len(mine)],
                )
            )
        for c in mine:
            c.start()
        copies.append(mine)
    leaving = []
    for i in range(3):
        for c in copies[i]:
            c.wait()
        for u in range(no):
            halves = []
            for h in range(2):
                odd = lax.rem(share[2 * (o0 + u) + h], 2) == 1
                rows = pairs[i, u, h].astype(jnp.float32)
                halves.append(jnp.where(odd, rows[8:], rows[:8]))
            stage[i, nd + u] = jnp.concatenate(halves, 0).astype(jnp.bfloat16)
        c = pltpu.make_async_copy(stage.at[i], sends[i], gone.at[i])
        c.start()
        leaving.append(c)
    for c in leaving:
        c.wait()


def pick(part, share, ranks, here, role, out_weight, down_weight):
    o0, no, d0, nd = part
    n = no + nd
    shape = (n, UNIT, LOCAL)
    return pl.pallas_call(
        functools.partial(pick_kernel, part),
        grid_spec=pltpu.PrefetchScalarGridSpec(
            num_scalar_prefetch=4,
            grid=(),
            in_specs=[pl.BlockSpec(memory_space=pltpu.HBM)] * 2,
            out_specs=[pl.BlockSpec(memory_space=pltpu.HBM)] * 3,
            scratch_shapes=[
                pltpu.VMEM((3, max(no, 1), 2, UNIT, LOCAL), jnp.bfloat16),
                pltpu.VMEM((3,) + shape, jnp.bfloat16),
                pltpu.SemaphoreType.DMA((3, 2 * no + nd)),
                pltpu.SemaphoreType.DMA((3,)),
            ],
        ),
        out_shape=[jax.ShapeDtypeStruct(shape, jnp.bfloat16)] * 3,
        compiler_params=pltpu.CompilerParams(vmem_limit_bytes=VMEM),
        cost_estimate=pl.CostEstimate(
            flops=0, bytes_accessed=9 * math.prod(shape) * 2, transcendentals=0
        ),
        name="pick_rows",
    )(share, ranks, here, role, out_weight, down_weight)


def spread(shards_in, rot, work):
    for at, x in shards_in:
        stack = jnp.concatenate(
            [x[:, c * 256 : (c + 1) * 256] for c in range(BLOCKS // 2)], 0
        )
        y = jnp.dot(stack, rot, preferred_element_type=jnp.float32)
        parts = butterflies(
            y[c * UNIT : (c + 1) * UNIT, h * SIDE : (h + 1) * SIDE]
            for c in range(BLOCKS // 2)
            for h in range(2)
        )
        for k in range(BLOCKS):
            work[at * BLOCKS + k] = parts[k]


def finish(quant, scales, work):
    lane = lax.broadcasted_iota(jnp.int32, (UNIT, SIDE), 1)
    top = jnp.zeros((UNIT, SIDE), jnp.float32)
    for k in range(BLOCKS):
        parts = butterflies(work[f * BLOCKS + k] for f in range(SHARDS))
        for f in range(SHARDS):
            a = f * BLOCKS + k
            m = jnp.max(jnp.abs(parts[f]), axis=1, keepdims=True)
            s = (m + 1e-06).astype(jnp.bfloat16).astype(jnp.float32)
            quant[:, a * SIDE : (a + 1) * SIDE] = (parts[f] * (1.0 / s)).astype(
                jnp.bfloat16
            )
            top = jnp.where(lane == a, m, top)
    scales[...] = (top + 1e-06).astype(jnp.bfloat16)


def rotate_kernel(part, n_alias, f_ref, r_ref, *refs):
    o0, no, d0, nd = part
    n = no + nd
    messages, local, rot_ref = refs[:4], refs[4], refs[5]
    outs = list(refs[6 + n_alias : -6])
    quants, tops, even, odd, left, left_top = refs[-6:]
    kinds = []
    if nd:
        kinds.append((0, nd, d0, outs.pop(0), outs.pop(0)))
    if no:
        kinds.append((nd, no, o0, outs.pop(0), outs.pop(0)))
    here, role = f_ref[0], r_ref[0]

    rot = rot_ref[...]
    places = []
    for m in range(8):
        of, slot = role ^ (m // 2), m % 2
        gap = (of == 3) & (slot == 1)
        at = shard_at(here, of, slot, False)
        places.append((m // 2, slot, gap, jnp.where(gap, here, at) if slot else at))

    def take(t, work):
        shards_in = []
        for m, slot, gap, at in places:
            x = messages[m][slot * n + t]
            if slot:
                x = jnp.where(gap, local[t], x)
            shards_in.append((at, x))
        spread(shards_in, rot, work)

    def leave(t, begin):
        for first, count, row, quant, scales in kinds:

            @pl.when((t >= first) & (t < first + count))
            def _():
                rows = pl.ds(pl.multiple_of((row + t - first) * UNIT, UNIT), UNIT)
                for c in (
                    pltpu.make_async_copy(quants.at[t], quant.at[rows, :], left.at[t]),
                    pltpu.make_async_copy(
                        tops.at[t], scales.at[rows, :], left_top.at[t]
                    ),
                ):
                    c.start() if begin else c.wait()

    def give(t, work):
        finish(quants.at[t], tops.at[t], work)

    take(0, even)

    def pair(j, _):
        t = 2 * j
        take(t + 1, odd)
        give(t, even)
        leave(t, True)

        @pl.when(t + 2 < n)
        def _():
            take(t + 2, even)
            give(t + 1, odd)

        @pl.when(t + 2 >= n)
        def _():
            give(t + 1, odd)

        leave(t + 1, True)
        return 0

    lax.fori_loop(0, n // 2, pair, 0)

    def settle(t, _):
        leave(t, False)
        return 0

    lax.fori_loop(0, n, settle, 0)


def rotate(part, messages, local, here, role, rot, before):
    o0, no, d0, nd = part
    n = no + nd
    columns = SHARDS * LOCAL
    shapes = [(128, columns), (128, SIDE), (256, columns), (256, SIDE)]
    used = [i for i in (2, 3, 0, 1) if (no, no, nd, nd)[i]]
    operands = list(messages) + [local, rot]
    aliases = {}
    for i, t in enumerate(used):
        if before[t] is not None:
            aliases[2 + len(operands)] = i
            operands.append(before[t])
    hbm = pl.BlockSpec(memory_space=pltpu.HBM)
    in_specs = [hbm] * len(operands)
    in_specs[:6] = [pl.BlockSpec(memory_space=pltpu.VMEM)] * 6
    elements = n * UNIT * columns
    work = pltpu.VMEM((SHARDS * BLOCKS, UNIT, SIDE), jnp.float32)
    results = pl.pallas_call(
        functools.partial(rotate_kernel, part, len(aliases)),
        grid_spec=pltpu.PrefetchScalarGridSpec(
            num_scalar_prefetch=2,
            grid=(),
            in_specs=in_specs,
            out_specs=[hbm] * len(used),
            scratch_shapes=[
                pltpu.VMEM((n, UNIT, columns), jnp.bfloat16),
                pltpu.VMEM((n, UNIT, SIDE), jnp.bfloat16),
                work,
                work,
                pltpu.SemaphoreType.DMA((n,)),
                pltpu.SemaphoreType.DMA((n,)),
            ],
        ),
        out_shape=[jax.ShapeDtypeStruct(shapes[t], jnp.bfloat16) for t in used],
        input_output_aliases=aliases,
        compiler_params=pltpu.CompilerParams(vmem_limit_bytes=24 * 2**20),
        cost_estimate=pl.CostEstimate(
            flops=elements * 256, bytes_accessed=elements * 4, transcendentals=0
        ),
        name="rotate_cast",
    )(here, role, *operands)
    after = list(before)
    for t, r in zip(used, results):
        after[t] = r
    return after


def pairs_of(target):
    def index(yl, z, yh, x, c):
        return (yl * 4 + z) * 16 + (yh * 4 + x) * 2 + c

    return [
        (index(*d), index(*target(*d)))
        for d in itertools.product(range(2), range(4), range(2), range(4), range(2))
    ]


def fetch_pairs(slot, flipped):
    def target(yl, z, yh, x, c):
        dy, dz, dh = FETCH[(x % 2 ^ flipped) * 2 + c][slot] or (0, 0, 0)
        return yl ^ dy, (z - dz) % 4, yh ^ dh, x, c

    return pairs_of(target)


OTHER = pairs_of(lambda yl, z, yh, x, c: (yl, z, yh, x, 1 - c))
ALONG = pairs_of(lambda yl, z, yh, x, c: (yl, z, yh, (x + 1 + 2 * c) % 4, c))
AXES = ("fsdp", "replica")


def shards(out_weight, down_weight, layer_share, rank_map):
    here = lax.axis_index("fsdp").astype(jnp.int32)[None]
    seat = (lax.axis_index("replica") % 4).astype(jnp.int32)[None]
    roles = [seat ^ 2 * f for f in FLIPPED]
    rot = two_blocks()
    picked = [
        pick(part, layer_share, rank_map, here, role, out_weight, down_weight)
        for part, role in zip(PARTS, roles)
    ]

    def fetch(k, sends):
        return [
            lax.ppermute(m, AXES, fetch_pairs(s, FLIPPED[k]))
            for s, m in enumerate(sends)
        ]

    def onward(message):
        return lax.ppermute(message, AXES, ALONG)

    def swap(message):
        return lax.ppermute(message, AXES, OTHER)

    def turn(k, messages, done):
        return rotate(PARTS[k], messages, picked[k][2], here, roles[k], rot, done)

    def tied(value, *others):
        return lax.optimization_barrier((value, *others))[0]

    done = [None] * 4
    own0 = fetch(0, picked[0][:2])
    own1 = fetch(1, picked[1][:2])
    own0 = jnp.concatenate(own0)
    own0 = tied(own0, *picked[2])
    along0 = onward(own0)
    other0 = swap(own0)
    own2 = fetch(2, [tied(m, own0) for m in picked[2][:2]])
    own1 = jnp.concatenate(own1)
    along1 = onward(own1)
    other1 = swap(own1)
    along_other0 = swap(tied(along0, own1))
    done = turn(0, [own0, other0, along0, along_other0], done)
    along_other1 = swap(tied(along1, done[2]))
    own2 = jnp.concatenate([tied(m, done[2]) for m in own2])
    along2 = onward(own2)
    other2 = swap(own2)
    done = turn(1, [own1, other1, along1, along_other1], done)
    along_other2 = swap(tied(along2, done[2]))
    done = turn(2, [own2, other2, along2, along_other2], done)
    return tuple(d[None] for d in done)


def solution(mesh):
    return jax.shard_map(
        shards,
        mesh=mesh,
        in_specs=(P(None, None, "fsdp"), P(None, None, "fsdp"), P(), P()),
        out_specs=(P("fsdp", None, None),) * 4,
        check_vma=False,
    )
```

```python
import functools
import itertools
import math

import jax
import jax.numpy as jnp
import numpy as np
from jax import lax
from jax.experimental import pallas as pl
from jax.experimental.pallas import tpu as pltpu
from jax.sharding import PartitionSpec as P

SIDE = 128
UNIT = 16
LOCAL = 2048
BLOCKS = LOCAL // SIDE
SHARDS = 8
PARTS = ((0, 0, 0, 8), (0, 2, 8, 8), (2, 6, 16, 0))
FLIPPED = (0, 0, 0)
FETCH = (
    ((0, 1, 0), (0, 3, 0)),
    ((1, 3, 0), (1, 1, 1)),
    ((0, 2, 0), (1, 2, 1)),
    ((1, 0, 0), None),
)
VMEM = 60 * 2**20


def signs(order):
    h = np.ones((1, 1), np.float32)
    while h.shape[0] < order:
        h = np.block([[h, h], [h, -h]])
    return h


def two_blocks():
    h = signs(SIDE)
    z = np.zeros_like(h)
    return jnp.asarray(np.block([[h, z], [z, h]]) / SIDE, jnp.bfloat16)


def butterflies(values):
    span = 1
    values = list(values)
    while span < len(values):
        for i in range(len(values)):
            if i & span == 0:
                lo, hi = values[i], values[i + span]
                values[i], values[i + span] = lo + hi, lo - hi
        span *= 2
    return values


def by_role(role, values):
    result = jnp.int32(values[3])
    for r in range(3):
        result = jnp.where(role == r, values[r], result)
    return result


def shard_at(here, role, slot, back):
    steps = [FETCH[r][slot] or (0, 0, 0) for r in range(4)]
    dy = by_role(role, [s[0] for s in steps])
    dz = by_role(role, [(4 - s[1]) % 4 if back else s[1] for s in steps])
    return ((here // 4) ^ dy) * 4 + ((here + dz) & 3)


def pick_kernel(part, share, ranks, f_ref, r_ref, out_hbm, down_hbm, *refs):
    o0, no, d0, nd = part
    n = no + nd
    sends, (pairs, stage, sems, gone) = refs[:3], refs[3:]
    here, role = f_ref[0], r_ref[0]
    to = [shard_at(here, role, slot, True) for slot in range(2)] + [here]
    copies = []
    for i in range(3):
        rank = ranks[to[i]]
        mine = []
        for u in range(no):
            for h in range(2):
                block = share[2 * (o0 + u) + h]
                row = rank * 64 + lax.rem(block, 8) // 2 * 16
                mine.append(
                    pltpu.make_async_copy(
                        out_hbm.at[block // 8, pl.ds(pl.multiple_of(row, 16), 16), :],
                        pairs.at[i, u, h],
                        sems.at[i, len(mine)],
                    )
                )
        for u in range(nd):
            block = share[d0 + u]
            row = rank * 128 + lax.rem(block, 8) * 16
            mine.append(
                pltpu.make_async_copy(
                    down_hbm.at[block // 8, pl.ds(pl.multiple_of(row, 16), 16), :],
                    stage.at[i, u],
                    sems.at[i, len(mine)],
                )
            )
        for c in mine:
            c.start()
        copies.append(mine)
    leaving = []
    for i in range(3):
        for c in copies[i]:
            c.wait()
        for u in range(no):
            halves = []
            for h in range(2):
                odd = lax.rem(share[2 * (o0 + u) + h], 2) == 1
                rows = pairs[i, u, h].astype(jnp.float32)
                halves.append(jnp.where(odd, rows[8:], rows[:8]))
            stage[i, nd + u] = jnp.concatenate(halves, 0).astype(jnp.bfloat16)
        c = pltpu.make_async_copy(stage.at[i], sends[i], gone.at[i])
        c.start()
        leaving.append(c)
    for c in leaving:
        c.wait()


def pick(part, share, ranks, here, role, out_weight, down_weight):
    o0, no, d0, nd = part
    n = no + nd
    shape = (n, UNIT, LOCAL)
    return pl.pallas_call(
        functools.partial(pick_kernel, part),
        grid_spec=pltpu.PrefetchScalarGridSpec(
            num_scalar_prefetch=4,
            grid=(),
            in_specs=[pl.BlockSpec(memory_space=pltpu.HBM)] * 2,
            out_specs=[pl.BlockSpec(memory_space=pltpu.HBM)] * 3,
            scratch_shapes=[
                pltpu.VMEM((3, max(no, 1), 2, UNIT, LOCAL), jnp.bfloat16),
                pltpu.VMEM((3,) + shape, jnp.bfloat16),
                pltpu.SemaphoreType.DMA((3, 2 * no + nd)),
                pltpu.SemaphoreType.DMA((3,)),
            ],
        ),
        out_shape=[jax.ShapeDtypeStruct(shape, jnp.bfloat16)] * 3,
        compiler_params=pltpu.CompilerParams(vmem_limit_bytes=VMEM),
        cost_estimate=pl.CostEstimate(
            flops=0, bytes_accessed=9 * math.prod(shape) * 2, transcendentals=0
        ),
        name="pick_rows",
    )(share, ranks, here, role, out_weight, down_weight)


def spread(shards_in, rot, work):
    for at, x in shards_in:
        stack = jnp.concatenate(
            [x[:, c * 256 : (c + 1) * 256] for c in range(BLOCKS // 2)], 0
        )
        y = jnp.dot(stack, rot, preferred_element_type=jnp.float32)
        parts = butterflies(
            y[c * UNIT : (c + 1) * UNIT, h * SIDE : (h + 1) * SIDE]
            for c in range(BLOCKS // 2)
            for h in range(2)
        )
        for k in range(BLOCKS):
            work[at * BLOCKS + k] = parts[k]


def finish(quant, scales, work):
    lane = lax.broadcasted_iota(jnp.int32, (UNIT, SIDE), 1)
    top = jnp.zeros((UNIT, SIDE), jnp.float32)
    for k in range(BLOCKS):
        parts = butterflies(work[f * BLOCKS + k] for f in range(SHARDS))
        for f in range(SHARDS):
            a = f * BLOCKS + k
            m = jnp.max(jnp.abs(parts[f]), axis=1, keepdims=True)
            s = (m + 1e-06).astype(jnp.bfloat16).astype(jnp.float32)
            quant[:, a * SIDE : (a + 1) * SIDE] = (parts[f] * (1.0 / s)).astype(
                jnp.bfloat16
            )
            top = jnp.where(lane == a, m, top)
    scales[...] = (top + 1e-06).astype(jnp.bfloat16)


def rotate_kernel(part, n_alias, f_ref, r_ref, *refs):
    o0, no, d0, nd = part
    n = no + nd
    messages, local, rot_ref = refs[:4], refs[4], refs[5]
    outs = list(refs[6 + n_alias : -6])
    quants, tops, even, odd, left, left_top = refs[-6:]
    kinds = []
    if nd:
        kinds.append((0, nd, d0, outs.pop(0), outs.pop(0)))
    if no:
        kinds.append((nd, no, o0, outs.pop(0), outs.pop(0)))
    here, role = f_ref[0], r_ref[0]

    rot = rot_ref[...]
    places = []
    for m in range(8):
        of, slot = role ^ (m // 2), m % 2
        gap = (of == 3) & (slot == 1)
        at = shard_at(here, of, slot, False)
        places.append((m // 2, slot, gap, jnp.where(gap, here, at) if slot else at))

    def take(t, work):
        shards_in = []
        for m, slot, gap, at in places:
            x = messages[m][slot * n + t]
            if slot:
                x = jnp.where(gap, local[t], x)
            shards_in.append((at, x))
        spread(shards_in, rot, work)

    def leave(t, begin):
        for first, count, row, quant, scales in kinds:

            @pl.when((t >= first) & (t < first + count))
            def _():
                rows = pl.ds(pl.multiple_of((row + t - first) * UNIT, UNIT), UNIT)
                for c in (
                    pltpu.make_async_copy(quants.at[t], quant.at[rows, :], left.at[t]),
                    pltpu.make_async_copy(
                        tops.at[t], scales.at[rows, :], left_top.at[t]
                    ),
                ):
                    c.start() if begin else c.wait()

    def give(t, work):
        finish(quants.at[t], tops.at[t], work)

    take(0, even)

    def pair(j, _):
        t = 2 * j
        take(t + 1, odd)
        give(t, even)
        leave(t, True)

        @pl.when(t + 2 < n)
        def _():
            take(t + 2, even)
            give(t + 1, odd)

        @pl.when(t + 2 >= n)
        def _():
            give(t + 1, odd)

        leave(t + 1, True)
        return 0

    lax.fori_loop(0, n // 2, pair, 0)

    def settle(t, _):
        leave(t, False)
        return 0

    lax.fori_loop(0, n, settle, 0)


def rotate(part, messages, local, here, role, rot, before):
    o0, no, d0, nd = part
    n = no + nd
    columns = SHARDS * LOCAL
    shapes = [(128, columns), (128, SIDE), (256, columns), (256, SIDE)]
    used = [i for i in (2, 3, 0, 1) if (no, no, nd, nd)[i]]
    operands = list(messages) + [local, rot]
    aliases = {}
    for i, t in enumerate(used):
        if before[t] is not None:
            aliases[2 + len(operands)] = i
            operands.append(before[t])
    hbm = pl.BlockSpec(memory_space=pltpu.HBM)
    in_specs = [hbm] * len(operands)
    in_specs[:6] = [pl.BlockSpec(memory_space=pltpu.VMEM)] * 6
    elements = n * UNIT * columns
    work = pltpu.VMEM((SHARDS * BLOCKS, UNIT, SIDE), jnp.float32)
    results = pl.pallas_call(
        functools.partial(rotate_kernel, part, len(aliases)),
        grid_spec=pltpu.PrefetchScalarGridSpec(
            num_scalar_prefetch=2,
            grid=(),
            in_specs=in_specs,
            out_specs=[hbm] * len(used),
            scratch_shapes=[
                pltpu.VMEM((n, UNIT, columns), jnp.bfloat16),
                pltpu.VMEM((n, UNIT, SIDE), jnp.bfloat16),
                work,
                work,
                pltpu.SemaphoreType.DMA((n,)),
                pltpu.SemaphoreType.DMA((n,)),
            ],
        ),
        out_shape=[jax.ShapeDtypeStruct(shapes[t], jnp.bfloat16) for t in used],
        input_output_aliases=aliases,
        compiler_params=pltpu.CompilerParams(vmem_limit_bytes=24 * 2**20),
        cost_estimate=pl.CostEstimate(
            flops=elements * 256, bytes_accessed=elements * 4, transcendentals=0
        ),
        name="rotate_cast",
    )(here, role, *operands)
    after = list(before)
    for t, r in zip(used, results):
        after[t] = r
    return after


def pairs_of(target):
    def index(yl, z, yh, x, c):
        return (yl * 4 + z) * 16 + (yh * 4 + x) * 2 + c

    return [
        (index(*d), index(*target(*d)))
        for d in itertools.product(range(2), range(4), range(2), range(4), range(2))
    ]


def fetch_pairs(slot, flipped):
    def target(yl, z, yh, x, c):
        dy, dz, dh = FETCH[(x % 2 ^ flipped) * 2 + c][slot] or (0, 0, 0)
        return yl ^ dy, (z - dz) % 4, yh ^ dh, x, c

    return pairs_of(target)


OTHER = pairs_of(lambda yl, z, yh, x, c: (yl, z, yh, x, 1 - c))
ALONG = pairs_of(lambda yl, z, yh, x, c: (yl, z, yh, (x + 1 + 2 * c) % 4, c))
BACK = pairs_of(lambda yl, z, yh, x, c: (yl, z, yh, (x + 3 - 2 * c) % 4, c))
AXES = ("fsdp", "replica")


def shards(out_weight, down_weight, layer_share, rank_map):
    here = lax.axis_index("fsdp").astype(jnp.int32)[None]
    seat = (lax.axis_index("replica") % 4).astype(jnp.int32)[None]
    roles = [seat ^ 2 * f for f in FLIPPED]
    rot = two_blocks()
    picked = [
        pick(part, layer_share, rank_map, here, role, out_weight, down_weight)
        for part, role in zip(PARTS, roles)
    ]

    def fetch(k, sends):
        return [
            lax.ppermute(m, AXES, fetch_pairs(s, FLIPPED[k]))
            for s, m in enumerate(sends)
        ]

    def onward(message, pairs=ALONG):
        return lax.ppermute(message, AXES, pairs)

    def swap(message):
        return lax.ppermute(message, AXES, OTHER)

    def turn(k, messages, done):
        return rotate(PARTS[k], messages, picked[k][2], here, roles[k], rot, done)

    def tied(value, *others):
        return lax.optimization_barrier((value, *others))[0]

    done = [None] * 4
    own0 = fetch(0, picked[0][:2])
    own1 = fetch(1, picked[1][:2])
    own0 = jnp.concatenate(own0)
    own0 = tied(own0, *picked[2])
    along0 = onward(own0)
    own2 = fetch(2, [tied(m, own0) for m in picked[2][:2]])
    own1 = jnp.concatenate(own1)
    along1 = onward(own1)
    other0 = swap(own0)
    other1 = swap(own1)
    along_other0 = swap(tied(along0, *own2))
    done = turn(0, [own0, other0, along0, along_other0], done)
    own2 = jnp.concatenate([tied(m, done[2]) for m in own2])
    along2 = onward(own2, BACK)
    other2 = swap(own2)
    along_other1 = swap(tied(along1, done[2]))
    done = turn(1, [own1, other1, along1, along_other1], done)
    along_other2 = swap(tied(along2, done[2]))
    done = turn(2, [own2, other2, along2, along_other2], done)
    return tuple(d[None] for d in done)


def solution(mesh):
    return jax.shard_map(
        shards,
        mesh=mesh,
        in_specs=(P(None, None, "fsdp"), P(None, None, "fsdp"), P(), P()),
        out_specs=(P("fsdp", None, None),) * 4,
        check_vma=False,
    )
```

```python
import functools
import itertools
import math

import jax
import jax.numpy as jnp
import numpy as np
from jax import lax
from jax.experimental import pallas as pl
from jax.experimental.pallas import tpu as pltpu
from jax.sharding import PartitionSpec as P

SIDE = 128
UNIT = 16
LOCAL = 2048
BLOCKS = LOCAL // SIDE
SHARDS = 8
PARTS = ((0, 0, 0, 8), (0, 2, 8, 8), (2, 6, 16, 0))
FLIPPED = (0, 0, 0)
FETCH = (
    ((0, 1, 0), (0, 3, 0)),
    ((1, 3, 0), (1, 1, 1)),
    ((0, 2, 0), (1, 2, 1)),
    ((1, 0, 0), None),
)
VMEM = 60 * 2**20


def signs(order):
    h = np.ones((1, 1), np.float32)
    while h.shape[0] < order:
        h = np.block([[h, h], [h, -h]])
    return h


def two_blocks():
    h = signs(SIDE)
    z = np.zeros_like(h)
    return jnp.asarray(np.block([[h, z], [z, h]]) / SIDE, jnp.bfloat16)


def butterflies(values):
    span = 1
    values = list(values)
    while span < len(values):
        for i in range(len(values)):
            if i & span == 0:
                lo, hi = values[i], values[i + span]
                values[i], values[i + span] = lo + hi, lo - hi
        span *= 2
    return values


def by_role(role, values):
    result = jnp.int32(values[3])
    for r in range(3):
        result = jnp.where(role == r, values[r], result)
    return result


def shard_at(here, role, slot, back):
    steps = [FETCH[r][slot] or (0, 0, 0) for r in range(4)]
    dy = by_role(role, [s[0] for s in steps])
    dz = by_role(role, [(4 - s[1]) % 4 if back else s[1] for s in steps])
    return ((here // 4) ^ dy) * 4 + ((here + dz) & 3)


def pick_kernel(part, which, share, ranks, f_ref, r_ref, out_hbm, down_hbm, *refs):
    o0, no, d0, nd = part
    n = no + nd
    kinds = len(which)
    sends, (pairs, stage, sems, gone) = refs[:kinds], refs[kinds:]
    here, role = f_ref[0], r_ref[0]
    to = [shard_at(here, role, slot, True) if slot < 2 else here for slot in which]
    copies = []
    for i in range(kinds):
        rank = ranks[to[i]]
        mine = []
        for u in range(no):
            for h in range(2):
                block = share[2 * (o0 + u) + h]
                row = rank * 64 + lax.rem(block, 8) // 2 * 16
                mine.append(
                    pltpu.make_async_copy(
                        out_hbm.at[block // 8, pl.ds(pl.multiple_of(row, 16), 16), :],
                        pairs.at[i, u, h],
                        sems.at[i, len(mine)],
                    )
                )
        for u in range(nd):
            block = share[d0 + u]
            row = rank * 128 + lax.rem(block, 8) * 16
            mine.append(
                pltpu.make_async_copy(
                    down_hbm.at[block // 8, pl.ds(pl.multiple_of(row, 16), 16), :],
                    stage.at[i, u],
                    sems.at[i, len(mine)],
                )
            )
        for c in mine:
            c.start()
        copies.append(mine)
    leaving = []
    for i in range(kinds):
        for c in copies[i]:
            c.wait()
        for u in range(no):
            halves = []
            for h in range(2):
                odd = lax.rem(share[2 * (o0 + u) + h], 2) == 1
                rows = pairs[i, u, h].astype(jnp.float32)
                halves.append(jnp.where(odd, rows[8:], rows[:8]))
            stage[i, nd + u] = jnp.concatenate(halves, 0).astype(jnp.bfloat16)
        c = pltpu.make_async_copy(stage.at[i], sends[i], gone.at[i])
        c.start()
        leaving.append(c)
    for c in leaving:
        c.wait()


def pick(part, which, share, ranks, here, role, out_weight, down_weight):
    o0, no, d0, nd = part
    n = no + nd
    shape = (n, UNIT, LOCAL)
    kinds = len(which)
    return pl.pallas_call(
        functools.partial(pick_kernel, part, which),
        grid_spec=pltpu.PrefetchScalarGridSpec(
            num_scalar_prefetch=4,
            grid=(),
            in_specs=[pl.BlockSpec(memory_space=pltpu.HBM)] * 2,
            out_specs=[pl.BlockSpec(memory_space=pltpu.HBM)] * kinds,
            scratch_shapes=[
                pltpu.VMEM((kinds, max(no, 1), 2, UNIT, LOCAL), jnp.bfloat16),
                pltpu.VMEM((kinds,) + shape, jnp.bfloat16),
                pltpu.SemaphoreType.DMA((kinds, 2 * no + nd)),
                pltpu.SemaphoreType.DMA((kinds,)),
            ],
        ),
        out_shape=[jax.ShapeDtypeStruct(shape, jnp.bfloat16)] * kinds,
        compiler_params=pltpu.CompilerParams(vmem_limit_bytes=VMEM),
        cost_estimate=pl.CostEstimate(
            flops=0, bytes_accessed=9 * math.prod(shape) * 2, transcendentals=0
        ),
        name="pick_rows",
    )(share, ranks, here, role, out_weight, down_weight)


def spread(shards_in, rot, work):
    for at, x in shards_in:
        stack = jnp.concatenate(
            [x[:, c * 256 : (c + 1) * 256] for c in range(BLOCKS // 2)], 0
        )
        y = jnp.dot(stack, rot, preferred_element_type=jnp.float32)
        parts = butterflies(
            y[c * UNIT : (c + 1) * UNIT, h * SIDE : (h + 1) * SIDE]
            for c in range(BLOCKS // 2)
            for h in range(2)
        )
        for k in range(BLOCKS):
            work[at * BLOCKS + k] = parts[k]


def finish(quant, scales, work):
    lane = lax.broadcasted_iota(jnp.int32, (UNIT, SIDE), 1)
    top = jnp.zeros((UNIT, SIDE), jnp.float32)
    for k in range(BLOCKS):
        parts = butterflies(work[f * BLOCKS + k] for f in range(SHARDS))
        for f in range(SHARDS):
            a = f * BLOCKS + k
            m = jnp.max(jnp.abs(parts[f]), axis=1, keepdims=True)
            s = (m + 1e-06).astype(jnp.bfloat16).astype(jnp.float32)
            quant[:, a * SIDE : (a + 1) * SIDE] = (parts[f] * (1.0 / s)).astype(
                jnp.bfloat16
            )
            top = jnp.where(lane == a, m, top)
    scales[...] = (top + 1e-06).astype(jnp.bfloat16)


def rotate_kernel(part, n_alias, f_ref, r_ref, *refs):
    o0, no, d0, nd = part
    n = no + nd
    messages, local, rot_ref = refs[:4], refs[4], refs[5]
    outs = list(refs[6 + n_alias : -6])
    quants, tops, even, odd, left, left_top = refs[-6:]
    kinds = []
    if nd:
        kinds.append((0, nd, d0, outs.pop(0), outs.pop(0)))
    if no:
        kinds.append((nd, no, o0, outs.pop(0), outs.pop(0)))
    here, role = f_ref[0], r_ref[0]

    rot = rot_ref[...]
    places = []
    for m in range(8):
        of, slot = role ^ (m // 2), m % 2
        gap = (of == 3) & (slot == 1)
        at = shard_at(here, of, slot, False)
        places.append((m // 2, slot, gap, jnp.where(gap, here, at) if slot else at))

    def take(t, work):
        shards_in = []
        for m, slot, gap, at in places:
            x = messages[m][slot * n + t]
            if slot:
                x = jnp.where(gap, local[t], x)
            shards_in.append((at, x))
        spread(shards_in, rot, work)

    def leave(t, begin):
        for first, count, row, quant, scales in kinds:

            @pl.when((t >= first) & (t < first + count))
            def _():
                rows = pl.ds(pl.multiple_of((row + t - first) * UNIT, UNIT), UNIT)
                for c in (
                    pltpu.make_async_copy(quants.at[t], quant.at[rows, :], left.at[t]),
                    pltpu.make_async_copy(
                        tops.at[t], scales.at[rows, :], left_top.at[t]
                    ),
                ):
                    c.start() if begin else c.wait()

    def give(t, work):
        finish(quants.at[t], tops.at[t], work)

    take(0, even)

    def pair(j, _):
        t = 2 * j
        take(t + 1, odd)
        give(t, even)
        leave(t, True)

        @pl.when(t + 2 < n)
        def _():
            take(t + 2, even)
            give(t + 1, odd)

        @pl.when(t + 2 >= n)
        def _():
            give(t + 1, odd)

        leave(t + 1, True)
        return 0

    lax.fori_loop(0, n // 2, pair, 0)

    def settle(t, _):
        leave(t, False)
        return 0

    lax.fori_loop(0, n, settle, 0)


def rotate(part, messages, local, here, role, rot, before):
    o0, no, d0, nd = part
    n = no + nd
    columns = SHARDS * LOCAL
    shapes = [(128, columns), (128, SIDE), (256, columns), (256, SIDE)]
    used = [i for i in (2, 3, 0, 1) if (no, no, nd, nd)[i]]
    operands = list(messages) + [local, rot]
    aliases = {}
    for i, t in enumerate(used):
        if before[t] is not None:
            aliases[2 + len(operands)] = i
            operands.append(before[t])
    hbm = pl.BlockSpec(memory_space=pltpu.HBM)
    in_specs = [hbm] * len(operands)
    in_specs[:6] = [pl.BlockSpec(memory_space=pltpu.VMEM)] * 6
    elements = n * UNIT * columns
    work = pltpu.VMEM((SHARDS * BLOCKS, UNIT, SIDE), jnp.float32)
    results = pl.pallas_call(
        functools.partial(rotate_kernel, part, len(aliases)),
        grid_spec=pltpu.PrefetchScalarGridSpec(
            num_scalar_prefetch=2,
            grid=(),
            in_specs=in_specs,
            out_specs=[hbm] * len(used),
            scratch_shapes=[
                pltpu.VMEM((n, UNIT, columns), jnp.bfloat16),
                pltpu.VMEM((n, UNIT, SIDE), jnp.bfloat16),
                work,
                work,
                pltpu.SemaphoreType.DMA((n,)),
                pltpu.SemaphoreType.DMA((n,)),
            ],
        ),
        out_shape=[jax.ShapeDtypeStruct(shapes[t], jnp.bfloat16) for t in used],
        input_output_aliases=aliases,
        compiler_params=pltpu.CompilerParams(vmem_limit_bytes=24 * 2**20),
        cost_estimate=pl.CostEstimate(
            flops=elements * 256, bytes_accessed=elements * 4, transcendentals=0
        ),
        name="rotate_cast",
    )(here, role, *operands)
    after = list(before)
    for t, r in zip(used, results):
        after[t] = r
    return after


def pairs_of(target):
    def index(yl, z, yh, x, c):
        return (yl * 4 + z) * 16 + (yh * 4 + x) * 2 + c

    return [
        (index(*d), index(*target(*d)))
        for d in itertools.product(range(2), range(4), range(2), range(4), range(2))
    ]


def fetch_pairs(slot, flipped):
    def target(yl, z, yh, x, c):
        dy, dz, dh = FETCH[(x % 2 ^ flipped) * 2 + c][slot] or (0, 0, 0)
        return yl ^ dy, (z - dz) % 4, yh ^ dh, x, c

    return pairs_of(target)


OTHER = pairs_of(lambda yl, z, yh, x, c: (yl, z, yh, x, 1 - c))
ALONG = pairs_of(lambda yl, z, yh, x, c: (yl, z, yh, (x + 1 + 2 * c) % 4, c))
BACK = pairs_of(lambda yl, z, yh, x, c: (yl, z, yh, (x + 3 - 2 * c) % 4, c))
AXES = ("fsdp", "replica")


def shards(out_weight, down_weight, layer_share, rank_map):
    here = lax.axis_index("fsdp").astype(jnp.int32)[None]
    seat = (lax.axis_index("replica") % 4).astype(jnp.int32)[None]
    roles = [seat ^ 2 * f for f in FLIPPED]
    rot = two_blocks()

    def choose(k, which):
        return list(
            pick(
                PARTS[k], which, layer_share, rank_map, here, roles[k], out_weight,
                down_weight,
            )
        )

    picked = [choose(0, (0, 1)), choose(1, (0, 1, 2)), choose(2, (0, 1, 2))]
    picked[0] += choose(0, (2,))

    def fetch(k, sends):
        return [
            lax.ppermute(m, AXES, fetch_pairs(s, FLIPPED[k]))
            for s, m in enumerate(sends)
        ]

    def onward(message, pairs=ALONG):
        return lax.ppermute(message, AXES, pairs)

    def swap(message):
        return lax.ppermute(message, AXES, OTHER)

    def turn(k, messages, done):
        return rotate(PARTS[k], messages, picked[k][2], here, roles[k], rot, done)

    def tied(value, *others):
        return lax.optimization_barrier((value, *others))[0]

    done = [None] * 4
    own0 = fetch(0, picked[0][:2])
    own1 = fetch(1, picked[1][:2])
    own0 = jnp.concatenate(own0)
    own0 = tied(own0, *picked[2], picked[0][2])
    along0 = onward(own0)
    own2 = fetch(2, [tied(m, own0) for m in picked[2][:2]])
    own1 = jnp.concatenate(own1)
    along1 = onward(own1)
    other0 = swap(own0)
    other1 = swap(own1)
    along_other0 = swap(tied(along0, *own2))
    done = turn(0, [own0, other0, along0, along_other0], done)
    own2 = jnp.concatenate([tied(m, done[2]) for m in own2])
    along2 = onward(own2, BACK)
    other2 = swap(own2)
    along_other1 = swap(tied(along1, done[2]))
    done = turn(1, [own1, other1, along1, along_other1], done)
    along_other2 = swap(tied(along2, done[2]))
    done = turn(2, [own2, other2, along2, along_other2], done)
    return tuple(d[None] for d in done)


def solution(mesh):
    return jax.shard_map(
        shards,
        mesh=mesh,
        in_specs=(P(None, None, "fsdp"), P(None, None, "fsdp"), P(), P()),
        out_specs=(P("fsdp", None, None),) * 4,
        check_vma=False,
    )
```
